32 devices in a mesh: lon: 8 (over z, y), head: 4 (over x, core).
Axes of the slice: x: 2, y: 2, z: 4, core: 2. Of those that a mesh axis runs over, the one named last changes fastest.
Arguments:
- tokens: bfloat16 [48, 128, 1024], P(None, ('lon', 'head')), may hold values from -6 to 6
- norm_gain: float32 [1024], replicated, may hold values from 0.25 to 1.75
- w_qkv: bfloat16 [1024, 3072], replicated, may hold values from -4 to 4
- w_out: bfloat16 [1024, 1024], replicated, may hold values from -0.1875 to 0.1875
- widths: int32 [6, 8], replicated, may hold values from 0 to 2, as said below
Outputs:
- mixed: bfloat16 [48, 128, 1024], P(None, ('lon', 'head'))
The draws below stay inside these ranges and needn't reach their ends.
Inputs may be any that keep to these rules, and one draw needn't show every extreme that they name: widths[b, c] is the longitude half-width in blocks of the neighbourhood of query block (b, c).
All inputs are finite; a program needn't handle non-finite values.
Results may differ from the reference program's by a relative error of at most 0.0092.
Values may be sent and summed in bfloat16 or wider, within the bound.
A program may use at most 64 MiB of HBM per device.

```python
import jax
import jax.numpy as jnp
from jax import lax

D = 1024
H = 8
HD = 128
LATITUDE_BANDS = 6
BLAT = 8
BLON = 16
BLOCK = 128
LAT = 48
NLON = 128
LONGITUDE_COUNT = 8
WIDEST_HALF_SPAN = 2


def draw_widths(key, part):
    key = jax.random.fold_in(key, 11)
    key_surplus, key_block_group, key_column_index = jax.random.split(key, 3)
    base = jnp.arange(LATITUDE_BANDS, dtype=jnp.int32) * WIDEST_HALF_SPAN // LATITUDE_BANDS
    extra = jax.random.randint(key_surplus, (LATITUDE_BANDS, LONGITUDE_COUNT), 0, max(WIDEST_HALF_SPAN // 3, 1) + 1)
    width_lookup = jnp.minimum(base[:, None] + extra, WIDEST_HALF_SPAN)
    block_group = jax.random.randint(key_block_group, (LATITUDE_BANDS, LONGITUDE_COUNT), 0, 6) == 0
    width_lookup = jnp.where(block_group, WIDEST_HALF_SPAN, width_lookup)
    chosen = jax.random.randint(key_column_index, (LATITUDE_BANDS,), 0, LONGITUDE_COUNT)
    column_ids = jnp.arange(LONGITUDE_COUNT, dtype=jnp.int32)
    width_lookup = jnp.where(column_ids[None, :] == chosen[:, None], WIDEST_HALF_SPAN, width_lookup)
    width_lookup = width_lookup.at[LATITUDE_BANDS - 1].set(WIDEST_HALF_SPAN)
    width_lookup = width_lookup.at[0, 0].set(0)
    return width_lookup.astype(jnp.int32)


def draw_tokens(key, part):
    key = jax.random.fold_in(key, 23)
    base = jnp.clip(jax.random.normal(key, (LAT, NLON, D), jnp.float32), -6.0, 6.0)
    return base.astype(jnp.bfloat16)


def draw_w_qkv(key, part):
    key = jax.random.fold_in(key, 37)
    drawn = jnp.clip(jax.random.normal(key, (D, 3 * D), jnp.float32), -6.0, 6.0)
    return (drawn * D ** (-0.5)).astype(jnp.bfloat16)


def centred(stream_key, dims, deviation, bound, held_as=jnp.bfloat16):
    values = jax.random.normal(stream_key, dims, jnp.float32) * deviation
    return jnp.minimum(jnp.maximum(values, -bound), bound).astype(held_as)


def setup_inputs(seed: int = 0) -> dict:
    key_of = jax.random.split(jax.random.key(seed), 6)
    tokens = draw_tokens(jax.random.fold_in(key_of[5], 71), 0)
    norm_gain = jnp.clip(1.0 + 0.15 * jax.random.normal(key_of[1], (D,), jnp.float32), 0.25, 1.75)
    w_qkv = draw_w_qkv(jax.random.fold_in(key_of[5], 71), 0)
    w_out = centred(key_of[3], (D, D), D ** -0.5, 0.1875)
    widths = draw_widths(jax.random.fold_in(key_of[5], 71), 0)
    return {"tokens": tokens, "norm_gain": norm_gain, "w_qkv": w_qkv, "w_out": w_out, "widths": widths}


def reference(tokens, norm_gain, w_qkv, w_out, widths):
    x32 = tokens.astype(jnp.float32)
    scale_rms = lax.rsqrt(lax.optimization_barrier(jnp.mean(x32 * x32, axis=-1, keepdims=True)) + 1e-05)
    normed = (x32 * scale_rms * norm_gain).astype(jnp.bfloat16)
    qkv = jnp.dot(normed.reshape(-1, D), w_qkv, preferred_element_type=jnp.float32).astype(jnp.bfloat16)
    qkv = qkv.reshape(LAT, NLON, 3, H, HD)
    window_extent = 2 * WIDEST_HALF_SPAN + 1
    offsets = jnp.arange(window_extent, dtype=jnp.int32) - WIDEST_HALF_SPAN
    scale = HD ** (-0.5)
    pieces = []
    for band in range(LATITUDE_BANDS):
        part = qkv[band * BLAT:(band + 1) * BLAT]
        blk = part.reshape(BLAT, LONGITUDE_COUNT, BLON, 3, H, HD).transpose(3, 4, 1, 0, 2, 5).reshape(3, H, LONGITUDE_COUNT, BLOCK, HD)
        query, keys, value_entries = (blk[0], blk[1], blk[2])
        kpad = jnp.concatenate([keys[:, LONGITUDE_COUNT - WIDEST_HALF_SPAN:], keys, keys[:, :WIDEST_HALF_SPAN]], axis=1)
        value_padded = jnp.concatenate([value_entries[:, LONGITUDE_COUNT - WIDEST_HALF_SPAN:], value_entries, value_entries[:, :WIDEST_HALF_SPAN]], axis=1)
        reach_row = widths[band]

        def one_block(column_position):
            kk = lax.dynamic_slice_in_dim(kpad, column_position, window_extent, 1).astype(jnp.float32)
            value_vectors = lax.dynamic_slice_in_dim(value_padded, column_position, window_extent, 1).astype(jnp.float32)
            qq = lax.dynamic_index_in_dim(query, column_position, 1, keepdims=False).astype(jnp.float32)
            scores = jnp.einsum('htd,hkud->htku', qq, kk) * scale
            allowed = (jnp.abs(offsets) <= reach_row[column_position])[None, None, :, None]
            top = lax.optimization_barrier(jnp.max(jnp.where(allowed, scores, -1e+30), axis=(2, 3), keepdims=True))
            expo = jnp.where(allowed, jnp.exp(scores - top), 0.0)
            total = lax.optimization_barrier(jnp.sum(expo, axis=(2, 3)))
            rounded = lax.optimization_barrier(expo.astype(jnp.bfloat16)).astype(jnp.float32)
            result = jnp.einsum('htku,hkud->htd', rounded, value_vectors) / total[..., None]
            return result.astype(jnp.bfloat16)
        res = lax.map(one_block, jnp.arange(LONGITUDE_COUNT, dtype=jnp.int32))
        res = res.reshape(LONGITUDE_COUNT, H, BLAT, BLON, HD).transpose(2, 0, 3, 1, 4).reshape(BLAT, NLON, D)
        pieces.append(res)
    attn = jnp.concatenate(pieces, axis=0)
    proj = jnp.dot(attn.reshape(-1, D), w_out, preferred_element_type=jnp.float32)
    return (x32.reshape(-1, D) + proj).astype(jnp.bfloat16).reshape(LAT, NLON, D)
```

```python
import jax
import jax.numpy as jnp
from jax import lax
from jax.experimental import pallas as pl
from jax.experimental.pallas import tpu as pltpu
from jax.sharding import PartitionSpec as P

H = 8
HD = 128
LATITUDE_BANDS = 6
BLAT = 8
BLON = 16
REACH = 2
D = H * HD
BLOCK = BLAT * BLON
GROUP = LATITUDE_BANDS // 2
CHUNK = BLOCK // 4
SLOTS = 2 * REACH + 1
MESH = pl.DeviceIdType.MESH


def shifted(array, axis, by):
    count = lax.axis_size(axis)
    return lax.ppermute(array, axis, [(i, (i + by) % count) for i in range(count)])


def per_device(tokens, norm_gain, w_qkv, w_out, widths):
    lat_rows, lon_tok, width = tokens.shape
    n_head = lax.axis_size("head")
    pairs = LATITUDE_BANDS * H // n_head
    sector = lon_tok * n_head
    sblocks = sector // BLON
    block_len = BLAT * BLON
    scale = HD ** (-0.5)
    x32 = tokens.astype(jnp.float32)
    scale_rms = lax.rsqrt(jnp.mean(x32 * x32, axis=-1, keepdims=True) + 1e-05)
    normed = (x32 * scale_rms * norm_gain).astype(jnp.bfloat16)
    qkv = jnp.dot(normed.reshape(-1, width), w_qkv, preferred_element_type=jnp.float32).astype(
        jnp.bfloat16
    )
    qkv = (
        qkv.reshape(LATITUDE_BANDS, BLAT, lon_tok, 3, H, HD)
        .transpose(0, 4, 1, 2, 3, 5)
        .reshape(LATITUDE_BANDS * H, BLAT, lon_tok, 3 * HD)
    )
    mine = lax.all_to_all(qkv, "head", split_axis=0, concat_axis=2, tiled=True)
    blocks = (
        mine.reshape(pairs, BLAT, sblocks, BLON, 3 * HD)
        .transpose(0, 2, 1, 3, 4)
        .reshape(pairs, sblocks, block_len, 3 * HD)
    )
    query = blocks[..., :HD]
    keyval = blocks[..., HD:]
    pair_ids = lax.axis_index("head") * pairs + jnp.arange(pairs, dtype=jnp.int32)
    band_ids = pair_ids // H
    onehot = (band_ids[:, None] == jnp.arange(LATITUDE_BANDS, dtype=jnp.int32)[None, :]).astype(
        jnp.int32
    )
    band_widths = jnp.sum(onehot[:, :, None] * widths[None, :, :], axis=1)
    reach = lax.dynamic_slice_in_dim(band_widths, lax.axis_index("lon") * sblocks, sblocks, 1)
    q_index = jnp.arange(sblocks, dtype=jnp.int32)

    def attend(state, pieces, shift_blocks):
        top, total, accum = state
        keys = pieces[..., :HD]
        value_entries = pieces[..., HD:]
        scores = (
            jnp.einsum("pqtd,pkud->pqtku", query, keys, preferred_element_type=jnp.float32) * scale
        )
        offset = shift_blocks + q_index[None, :] - q_index[:, None]
        allowed = jnp.abs(offset)[None, :, :] <= reach[:, :, None]
        allowed = allowed[:, :, None, :, None]
        new_top = jnp.maximum(top, jnp.max(jnp.where(allowed, scores, -1e30), axis=(3, 4)))
        expo = jnp.where(allowed, jnp.exp(scores - new_top[..., None, None]), 0.0)
        factor = jnp.exp(top - new_top)
        total = total * factor + jnp.sum(expo, axis=(3, 4))
        update = jnp.einsum(
            "pqtku,pkud->pqtd",
            expo.astype(jnp.bfloat16),
            value_entries,
            preferred_element_type=jnp.float32,
        )
        accum = accum * factor[..., None] + update
        return (new_top, total, accum)

    start = (
        jnp.full((pairs, sblocks, block_len), -1e30, jnp.float32),
        jnp.zeros((pairs, sblocks, block_len), jnp.float32),
        jnp.zeros((pairs, sblocks, block_len, HD), jnp.float32),
    )
    state = attend(start, keyval, 0)
    travel = shifted(keyval, "lon", -REACH)
    state = attend(state, travel, REACH * sblocks)
    for step in range(1, 2 * REACH + 1):
        travel = shifted(travel, "lon", 1)
        distance = REACH - step
        if distance != 0:
            state = attend(state, travel, distance * sblocks)
    top, total, accum = state
    result = (accum / total[..., None]).astype(jnp.bfloat16)
    result = (
        result.reshape(pairs, sblocks, BLAT, BLON, HD)
        .transpose(0, 2, 1, 3, 4)
        .reshape(pairs, BLAT, sector, HD)
    )
    back = lax.all_to_all(result, "head", split_axis=2, concat_axis=0, tiled=True)
    back = (
        back.reshape(LATITUDE_BANDS, H, BLAT, lon_tok, HD)
        .transpose(0, 2, 3, 1, 4)
        .reshape(lat_rows * lon_tok, width)
    )
    proj = jnp.dot(back, w_out, preferred_element_type=jnp.float32)
    return (x32.reshape(-1, width) + proj).astype(jnp.bfloat16).reshape(lat_rows, lon_tok, width)


def fused_kernel(
    tok_ref, gain_ref, wqkv_hbm, wout_hbm, widths_ref, out_ref,
    buf, stage, wq, wo, qs, kv, att, back,
    wsem, x_send, x_recv, o_send, o_recv, c_send, c_recv, r_send, r_recv,
):
    n_lon = lax.axis_size("lon")
    lon, head = lax.axis_index("lon"), lax.axis_index("head")
    x, core = head // 2, head % 2
    y = lon % 2
    turn = 2 * y - 1
    far = lax.rem(lon + 2 * turn + n_lon, n_lon)
    near = lax.rem(lon - 2 * turn + n_lon, n_lon)
    pair = lon - turn
    sibling = (lon, 2 * x + 1 - core)
    across = (lon, 2 * (1 - x) + core)
    diagonal = (lon, 2 * (1 - x) + 1 - core)
    partners = [sibling, across, diagonal, (far, head), (near, head), (pair, head)]
    half_cols = H // 2 * HD

    barrier = pltpu.get_barrier_semaphore()
    for where in partners:
        pl.semaphore_signal(barrier, inc=1, device_id=where, device_id_type=MESH)

    loads = []
    for i in range(3):
        cols = pl.ds(pl.multiple_of(i * H * HD + core * half_cols, 128), half_cols)
        loads.append(
            pltpu.make_async_copy(
                wqkv_hbm.at[:, cols], wq.at[:, pl.ds(i * half_cols, half_cols)], wsem.at[i]
            )
        )
    loads.append(pltpu.make_async_copy(wout_hbm, wo, wsem.at[3]))
    for load in loads:
        load.start()

    def normed(row):
        part = tok_ref[pl.ds(pl.multiple_of(row, CHUNK), CHUNK), :].astype(jnp.float32)
        inv = lax.rsqrt(jnp.mean(part * part, axis=-1, keepdims=True) + 1e-05)
        return (part * inv * gain_ref[...]).astype(jnp.bfloat16)

    def remote(src, dst, send, recv, where):
        return pltpu.make_async_remote_copy(
            src_ref=src, dst_ref=dst, send_sem=send, recv_sem=recv,
            device_id=where, device_id_type=MESH,
        )

    sent = []

    def begin(copy):
        copy.start()
        sent.append(copy)
        return copy

    x_copies = []
    for j in range(GROUP):
        stage[j] = normed(((1 - x) * GROUP + j) * CHUNK)
        if j == 0:
            pl.semaphore_wait(barrier, len(partners))
        x_copies.append(
            begin(remote(stage.at[j], buf.at[j, 0, core, x], x_send.at[j], x_recv.at[j], across))
        )
        buf[j, 0, core, x] = normed((x * GROUP + j) * CHUNK)

    def share(slot, j):
        half = buf.at[j, slot, core]
        return begin(remote(half, half, c_send.at[j, slot], c_recv.at[j, slot], sibling))

    def spread(j):
        x_copies[j].wait_recv()
        own = buf.at[j, 0, core]
        copies = {}
        for slot, where in ((3, (far, head)), (2, (near, head)), (1, (pair, head))):
            copies[slot] = begin(
                remote(
                    own, buf.at[j, slot, core], o_send.at[j, slot], o_recv.at[j, slot], where
                )
            )
        return copies, share(0, j)

    def project(j, first, count):
        rows = buf[j, first : first + count].reshape(count * 4 * CHUNK, D)
        made = jnp.dot(rows, wq[:, half_cols:], preferred_element_type=jnp.float32)
        kv[pl.ds(first * 4 * CHUNK, count * 4 * CHUNK), :] = made.astype(jnp.bfloat16)

    block = lax.broadcasted_iota(jnp.int32, (1, SLOTS * BLOCK), 1) // BLOCK
    distance = jnp.where(block == 0, 0, jnp.where((block == 1) | (block == 4), 1, 2))
    scale = HD ** (-0.5)

    pending, own_share = spread(0)
    returns = []
    for j in range(GROUP):
        arrive, shared0 = pending, own_share
        if j + 1 < GROUP:
            pending, own_share = None, None
        shared0.wait_recv()
        if j == 0:
            for load in loads[:3]:
                load.wait()
        rows = buf[j, 0].reshape(BLOCK, D)
        qs[...] = jnp.dot(rows, wq[:, :half_cols], preferred_element_type=jnp.float32).astype(
            jnp.bfloat16
        )
        project(j, 0, 1)
        arrive[3].wait_recv()
        held = buf.at[j, 3, core]
        relay = begin(
            remote(
                held, buf.at[j, 4, core], o_send.at[j, 4], o_recv.at[j, 4], (pair, head)
            )
        )
        shares = [share(3, j)]
        if j + 1 < GROUP:
            pending, own_share = spread(j + 1)
        arrive[1].wait_recv()
        shares.append(share(1, j))
        arrive[2].wait_recv()
        shares.append(share(2, j))
        for copy in shares:
            copy.wait_recv()
        project(j, 1, 3)
        relay.wait_recv()
        share(4, j).wait_recv()
        project(j, 4, 1)

        allowed = distance <= widths_ref[x * GROUP + j, lon]
        for h in range(H // 2):
            cols = pl.ds(h * HD, HD)
            scores = lax.dot_general(
                qs[:, cols], kv[:, cols], (((1,), (1,)), ((), ())),
                preferred_element_type=jnp.float32,
            )
            scores = jnp.where(allowed, scores * scale, -1e30)
            top = jnp.max(scores, axis=1, keepdims=True)
            expo = jnp.exp(scores - top)
            total = jnp.sum(expo, axis=1, keepdims=True)
            mixed = jnp.dot(
                expo.astype(jnp.bfloat16), kv[:, pl.ds(half_cols + h * HD, HD)],
                preferred_element_type=jnp.float32,
            )
            att[j, :, cols] = (mixed / total).astype(jnp.bfloat16)
        rows = pl.ds(pl.multiple_of((x * GROUP + j) * CHUNK, CHUNK), CHUNK)
        for kind, (where, to_x, to_core) in enumerate(
            ((across, 1 - x, core), (diagonal, 1 - x, 1 - core), (sibling, x, 1 - core))
        ):
            piece = pl.ds(pl.multiple_of((to_core * 2 + to_x) * CHUNK, CHUNK), CHUNK)
            returns.append(
                begin(
                    remote(
                        att.at[j, piece], back.at[core, rows],
                        r_send.at[j, kind], r_recv.at[j, kind], where,
                    )
                )
            )
        mine = pl.ds(pl.multiple_of((core * 2 + x) * CHUNK, CHUNK), CHUNK)
        back[core, rows] = att[j, mine]

    loads[3].wait()
    for copy in returns:
        copy.wait_recv()
    proj = jnp.dot(back[0], wo[:half_cols], preferred_element_type=jnp.float32)
    proj += jnp.dot(back[1], wo[half_cols:], preferred_element_type=jnp.float32)
    out_ref[...] = (tok_ref[...].astype(jnp.float32) + proj).astype(jnp.bfloat16)
    for copy in sent:
        copy.wait_send()


def fused_device(tokens, norm_gain, w_qkv, w_out, widths):
    lat_rows, lon_tok, width = tokens.shape
    count = lat_rows * lon_tok
    half_cols = H // 2 * HD
    dma = pltpu.SemaphoreType.DMA
    vmem = pl.BlockSpec(memory_space=pltpu.VMEM)
    hbm = pl.BlockSpec(memory_space=pl.ANY)
    out = pl.pallas_call(
        fused_kernel,
        out_shape=jax.ShapeDtypeStruct((count, width), jnp.bfloat16),
        in_specs=[vmem, vmem, hbm, hbm, pl.BlockSpec(memory_space=pltpu.SMEM)],
        out_specs=vmem,
        scratch_shapes=[
            pltpu.VMEM((GROUP, SLOTS, 2, 2, CHUNK, width), jnp.bfloat16),
            pltpu.VMEM((GROUP, CHUNK, width), jnp.bfloat16),
            pltpu.VMEM((width, 3 * half_cols), jnp.bfloat16),
            pltpu.VMEM((width, width), jnp.bfloat16),
            pltpu.VMEM((BLOCK, half_cols), jnp.bfloat16),
            pltpu.VMEM((SLOTS * BLOCK, 2 * half_cols), jnp.bfloat16),
            pltpu.VMEM((GROUP, BLOCK, half_cols), jnp.bfloat16),
            pltpu.VMEM((2, count, half_cols), jnp.bfloat16),
            dma((4,)),
            dma((GROUP,)),
            dma((GROUP,)),
            dma((GROUP, SLOTS)),
            dma((GROUP, SLOTS)),
            dma((GROUP, SLOTS)),
            dma((GROUP, SLOTS)),
            dma((GROUP, 3)),
            dma((GROUP, 3)),
        ],
        compiler_params=pltpu.CompilerParams(
            collective_id=0, has_side_effects=True, vmem_limit_bytes=48 * 1024 * 1024
        ),
    )(tokens.reshape(count, width), norm_gain.reshape(1, width), w_qkv, w_out, widths)
    return out.reshape(lat_rows, lon_tok, width)


def solution(mesh):
    placed = (P(None, ("lon", "head"), None), P(), P(), P(), P())
    one_block = mesh.shape["lon"] == 8 and mesh.shape["head"] == 4
    return jax.shard_map(
        fused_device if one_block else per_device,
        mesh=mesh,
        in_specs=placed,
        out_specs=P(None, ("lon", "head"), None),
        check_vma=False,
    )
```

```python
import jax
import jax.numpy as jnp
from jax import lax
from jax.experimental import pallas as pl
from jax.experimental.pallas import tpu as pltpu
from jax.sharding import PartitionSpec as P

H = 8
HD = 128
LATITUDE_BANDS = 6
BLAT = 8
BLON = 16
REACH = 2
D = H * HD
BLOCK = BLAT * BLON
GROUP = LATITUDE_BANDS // 2
CHUNK = BLOCK // 4
SLOTS = 2 * REACH + 1
MESH = pl.DeviceIdType.MESH


def shifted(array, axis, by):
    count = lax.axis_size(axis)
    return lax.ppermute(array, axis, [(i, (i + by) % count) for i in range(count)])


def per_device(tokens, norm_gain, w_qkv, w_out, widths):
    lat_rows, lon_tok, width = tokens.shape
    n_head = lax.axis_size("head")
    pairs = LATITUDE_BANDS * H // n_head
    sector = lon_tok * n_head
    sblocks = sector // BLON
    block_len = BLAT * BLON
    scale = HD ** (-0.5)
    x32 = tokens.astype(jnp.float32)
    scale_rms = lax.rsqrt(jnp.mean(x32 * x32, axis=-1, keepdims=True) + 1e-05)
    normed = (x32 * scale_rms * norm_gain).astype(jnp.bfloat16)
    qkv = jnp.dot(normed.reshape(-1, width), w_qkv, preferred_element_type=jnp.float32).astype(
        jnp.bfloat16
    )
    qkv = (
        qkv.reshape(LATITUDE_BANDS, BLAT, lon_tok, 3, H, HD)
        .transpose(0, 4, 1, 2, 3, 5)
        .reshape(LATITUDE_BANDS * H, BLAT, lon_tok, 3 * HD)
    )
    mine = lax.all_to_all(qkv, "head", split_axis=0, concat_axis=2, tiled=True)
    blocks = (
        mine.reshape(pairs, BLAT, sblocks, BLON, 3 * HD)
        .transpose(0, 2, 1, 3, 4)
        .reshape(pairs, sblocks, block_len, 3 * HD)
    )
    query = blocks[..., :HD]
    keyval = blocks[..., HD:]
    pair_ids = lax.axis_index("head") * pairs + jnp.arange(pairs, dtype=jnp.int32)
    band_ids = pair_ids // H
    onehot = (band_ids[:, None] == jnp.arange(LATITUDE_BANDS, dtype=jnp.int32)[None, :]).astype(
        jnp.int32
    )
    band_widths = jnp.sum(onehot[:, :, None] * widths[None, :, :], axis=1)
    reach = lax.dynamic_slice_in_dim(band_widths, lax.axis_index("lon") * sblocks, sblocks, 1)
    q_index = jnp.arange(sblocks, dtype=jnp.int32)

    def attend(state, pieces, shift_blocks):
        top, total, accum = state
        keys = pieces[..., :HD]
        value_entries = pieces[..., HD:]
        scores = (
            jnp.einsum("pqtd,pkud->pqtku", query, keys, preferred_element_type=jnp.float32) * scale
        )
        offset = shift_blocks + q_index[None, :] - q_index[:, None]
        allowed = jnp.abs(offset)[None, :, :] <= reach[:, :, None]
        allowed = allowed[:, :, None, :, None]
        new_top = jnp.maximum(top, jnp.max(jnp.where(allowed, scores, -1e30), axis=(3, 4)))
        expo = jnp.where(allowed, jnp.exp(scores - new_top[..., None, None]), 0.0)
        factor = jnp.exp(top - new_top)
        total = total * factor + jnp.sum(expo, axis=(3, 4))
        update = jnp.einsum(
            "pqtku,pkud->pqtd",
            expo.astype(jnp.bfloat16),
            value_entries,
            preferred_element_type=jnp.float32,
        )
        accum = accum * factor[..., None] + update
        return (new_top, total, accum)

    start = (
        jnp.full((pairs, sblocks, block_len), -1e30, jnp.float32),
        jnp.zeros((pairs, sblocks, block_len), jnp.float32),
        jnp.zeros((pairs, sblocks, block_len, HD), jnp.float32),
    )
    state = attend(start, keyval, 0)
    travel = shifted(keyval, "lon", -REACH)
    state = attend(state, travel, REACH * sblocks)
    for step in range(1, 2 * REACH + 1):
        travel = shifted(travel, "lon", 1)
        distance = REACH - step
        if distance != 0:
            state = attend(state, travel, distance * sblocks)
    top, total, accum = state
    result = (accum / total[..., None]).astype(jnp.bfloat16)
    result = (
        result.reshape(pairs, sblocks, BLAT, BLON, HD)
        .transpose(0, 2, 1, 3, 4)
        .reshape(pairs, BLAT, sector, HD)
    )
    back = lax.all_to_all(result, "head", split_axis=2, concat_axis=0, tiled=True)
    back = (
        back.reshape(LATITUDE_BANDS, H, BLAT, lon_tok, HD)
        .transpose(0, 2, 3, 1, 4)
        .reshape(lat_rows * lon_tok, width)
    )
    proj = jnp.dot(back, w_out, preferred_element_type=jnp.float32)
    return (x32.reshape(-1, width) + proj).astype(jnp.bfloat16).reshape(lat_rows, lon_tok, width)


def fused_kernel(
    tok_hbm, gain_hbm, wqkv_hbm, wout_hbm, widths_hbm, out_ref,
    tok, gain, reach, buf, stage, wq, wo, qs, kv, att, back,
    wsem, x_send, x_recv, o_send, o_recv, c_send, c_recv, r_send, r_recv,
):
    n_lon = lax.axis_size("lon")
    lon, head = lax.axis_index("lon"), lax.axis_index("head")
    x, core = head // 2, head % 2
    y = lon % 2
    turn = 2 * y - 1
    far = (lax.rem(lon + 2 * turn + n_lon, n_lon), head)
    near = (lax.rem(lon - 2 * turn + n_lon, n_lon), head)
    pair = (lon - turn, head)
    sibling = (lon, 2 * x + 1 - core)
    across = (lon, 2 * (1 - x) + core)
    diagonal = (lon, 2 * (1 - x) + 1 - core)
    partners = [sibling, across, diagonal, far, near, pair]
    half_cols = H // 2 * HD

    barrier = pltpu.get_barrier_semaphore()
    for where in partners:
        pl.semaphore_signal(barrier, inc=1, device_id=where, device_id_type=MESH)

    first = [
        pltpu.make_async_copy(tok_hbm, tok, wsem.at[4]),
        pltpu.make_async_copy(gain_hbm, gain, wsem.at[5]),
    ]
    loads = []
    for i in range(3):
        cols = pl.ds(pl.multiple_of(i * H * HD + core * half_cols, 128), half_cols)
        loads.append(
            pltpu.make_async_copy(
                wqkv_hbm.at[:, cols], wq.at[:, pl.ds(i * half_cols, half_cols)], wsem.at[i]
            )
        )
    loads.append(pltpu.make_async_copy(wout_hbm, wo, wsem.at[3]))
    loads.append(pltpu.make_async_copy(widths_hbm, reach, wsem.at[6]))
    for load in first + loads:
        load.start()
    for load in first:
        load.wait()

    def normed(band):
        part = tok[pl.ds(band * BLAT, BLAT)].astype(jnp.float32).reshape(CHUNK, D)
        inv = lax.rsqrt(jnp.mean(part * part, axis=-1, keepdims=True) + 1e-05)
        return (part * inv * gain[...]).astype(jnp.bfloat16)

    def remote(src, dst, send, recv, where):
        return pltpu.make_async_remote_copy(
            src_ref=src, dst_ref=dst, send_sem=send, recv_sem=recv,
            device_id=where, device_id_type=MESH,
        )

    sent = []

    def begin(copy):
        copy.start()
        sent.append(copy)
        return copy

    def at(slot, j, piece):
        return buf.at[slot, j, core, x if piece == 0 else 1 - x]

    def move(slot_from, slot_to, j, piece, where):
        return begin(
            remote(
                at(slot_from, j, piece), at(slot_to, j, piece),
                o_send.at[slot_to, j, piece], o_recv.at[slot_to, j, piece], where,
            )
        )

    def share(slot, j):
        half = buf.at[slot, j, core]
        return begin(remote(half, half, c_send.at[slot, j], c_recv.at[slot, j], sibling))

    moves = {}

    def spread(j, piece):
        for slot, where in ((3, far), (2, near), (1, pair)):
            moves[slot, j, piece] = move(0, slot, j, piece, where)

    crossing = []
    for j in range(GROUP):
        stage[j] = normed((1 - x) * GROUP + j)
        if j == 0:
            pl.semaphore_wait(barrier, len(partners))
        crossing.append(
            begin(remote(stage.at[j], buf.at[0, j, core, x], x_send.at[j], x_recv.at[j], across))
        )
        buf[0, j, core, x] = normed(x * GROUP + j)
        if j == 0:
            spread(0, 0)
    shares = []
    for j in range(GROUP):
        crossing[j].wait_recv()
        spread(j, 1)
        if j + 1 < GROUP:
            spread(j + 1, 0)
        shares.append(share(0, j))

    def project(slot, j, with_query):
        rows = jnp.concatenate(
            [buf[s, i].reshape(BLOCK, D) for s in slot for i in j], axis=0
        )
        start = 0 if with_query else half_cols
        made = jnp.dot(rows, wq[:, start:], preferred_element_type=jnp.float32).astype(
            jnp.bfloat16
        )
        n = 0
        for s in slot:
            for i in j:
                part = made[n * BLOCK : (n + 1) * BLOCK]
                if with_query:
                    qs[i] = part[:, :half_cols]
                    part = part[:, half_cols:]
                kv[i, pl.ds(s * BLOCK, BLOCK), :] = part
                n += 1

    for load in loads[:3]:
        load.wait()
    for copy in shares:
        copy.wait_recv()
    project((0,), range(GROUP), True)
    loads[4].wait()

    def relay(j):
        for piece in range(2):
            moves[3, j, piece].wait_recv()
            moves[4, j, piece] = move(3, 4, j, piece, pair)
        return share(3, j)

    def collect(slot, j):
        for piece in range(2):
            moves[slot, j, piece].wait_recv()
        return share(slot, j)

    def attend(j, h, low, high, dist):
        cols = pl.ds(h * HD, HD)
        rows = pl.ds(low * BLOCK, (high - low) * BLOCK)
        scores = lax.dot_general(
            qs[j, :, cols], kv[j, rows, cols], (((1,), (1,)), ((), ())),
            preferred_element_type=jnp.float32,
        )
        scores = jnp.where(dist <= reach[x * GROUP + j, lon], scores * HD ** (-0.5), -1e30)
        top = jnp.max(scores, axis=1, keepdims=True)

        def weigh(new_top):
            expo = jnp.exp(scores - new_top)
            value = jnp.dot(
                expo.astype(jnp.bfloat16), kv[j, rows, pl.ds(half_cols + h * HD, HD)],
                preferred_element_type=jnp.float32,
            )
            return jnp.sum(expo, axis=1, keepdims=True), value

        return top, weigh

    block = lax.broadcasted_iota(jnp.int32, (1, 4 * BLOCK), 1) // BLOCK
    dist_most = jnp.minimum(block, 2)
    dist_last = jnp.ones((1, BLOCK), jnp.int32)
    returns = {}

    def finish(js):
        bands = [chip * GROUP + j for chip in range(2) for j in js]
        for j in js:
            for copy in returns[j]:
                copy.wait_recv()
        rows = jnp.concatenate(
            [
                jnp.concatenate([back[c, b * CHUNK : (b + 1) * CHUNK] for b in bands], axis=0)
                for c in range(2)
            ],
            axis=1,
        )
        proj = jnp.dot(rows, wo[...], preferred_element_type=jnp.float32)
        for n, b in enumerate(bands):
            held = tok[b * BLAT : (b + 1) * BLAT].astype(jnp.float32)
            add = proj[n * CHUNK : (n + 1) * CHUNK].reshape(held.shape)
            out_ref[b * BLAT : (b + 1) * BLAT] = (held + add).astype(jnp.bfloat16)

    for j in range(GROUP):
        far_share = relay(j)
        if j == 0:
            early = [collect(1, i) for i in range(GROUP)]
            for copy in early:
                copy.wait_recv()
            project((1,), range(GROUP), False)
        near_share = collect(2, j)
        far_share.wait_recv()
        near_share.wait_recv()
        project((2, 3), (j,), False)
        states = []
        for h in range(H // 2):
            top, weigh = attend(j, h, 0, 4, dist_most)
            states.append((top, *weigh(top)))
        if j == GROUP - 1:
            loads[3].wait()
            finish(range(GROUP - 1))
        collect(4, j).wait_recv()
        project((4,), (j,), False)
        for h in range(H // 2):
            top, total, value = states[h]
            last_top, weigh = attend(j, h, 4, 5, dist_last)
            new_top = jnp.maximum(top, last_top)
            factor = jnp.exp(top - new_top)
            last_total, last_value = weigh(new_top)
            value = value * factor + last_value
            total = total * factor + last_total
            att[j, :, pl.ds(h * HD, HD)] = (value / total).astype(jnp.bfloat16)
        rows = pl.ds(pl.multiple_of((x * GROUP + j) * CHUNK, CHUNK), CHUNK)
        returns[j] = []
        for kind, (where, to_x, to_core) in enumerate(
            ((across, 1 - x, core), (diagonal, 1 - x, 1 - core), (sibling, x, 1 - core))
        ):
            piece = pl.ds(pl.multiple_of((to_core * 2 + to_x) * CHUNK, CHUNK), CHUNK)
            returns[j].append(
                begin(
                    remote(
                        att.at[j, piece], back.at[core, rows],
                        r_send.at[j, kind], r_recv.at[j, kind], where,
                    )
                )
            )
        mine = pl.ds(pl.multiple_of((core * 2 + x) * CHUNK, CHUNK), CHUNK)
        back[core, rows] = att[j, mine]

    finish((GROUP - 1,))
    for copy in sent:
        copy.wait_send()


def fused_device(tokens, norm_gain, w_qkv, w_out, widths):
    lat_rows, lon_tok, width = tokens.shape
    count = lat_rows * lon_tok
    half_cols = H // 2 * HD
    dma = pltpu.SemaphoreType.DMA
    hbm = pl.BlockSpec(memory_space=pltpu.HBM)
    return pl.pallas_call(
        fused_kernel,
        out_shape=jax.ShapeDtypeStruct(tokens.shape, jnp.bfloat16),
        in_specs=[hbm] * 5,
        out_specs=pl.BlockSpec(memory_space=pltpu.VMEM),
        scratch_shapes=[
            pltpu.VMEM(tokens.shape, jnp.bfloat16),
            pltpu.VMEM((1, width), jnp.float32),
            pltpu.SMEM(widths.shape, jnp.int32),
            pltpu.VMEM((SLOTS, GROUP, 2, 2, CHUNK, width), jnp.bfloat16),
            pltpu.VMEM((GROUP, CHUNK, width), jnp.bfloat16),
            pltpu.VMEM((width, 3 * half_cols), jnp.bfloat16),
            pltpu.VMEM((width, width), jnp.bfloat16),
            pltpu.VMEM((GROUP, BLOCK, half_cols), jnp.bfloat16),
            pltpu.VMEM((GROUP, SLOTS * BLOCK, 2 * half_cols), jnp.bfloat16),
            pltpu.VMEM((GROUP, BLOCK, half_cols), jnp.bfloat16),
            pltpu.VMEM((2, count, half_cols), jnp.bfloat16),
            dma((7,)),
            dma((GROUP,)),
            dma((GROUP,)),
            dma((SLOTS, GROUP, 2)),
            dma((SLOTS, GROUP, 2)),
            dma((SLOTS, GROUP)),
            dma((SLOTS, GROUP)),
            dma((GROUP, 3)),
            dma((GROUP, 3)),
        ],
        compiler_params=pltpu.CompilerParams(
            collective_id=0, has_side_effects=True, vmem_limit_bytes=56 * 1024 * 1024
        ),
    )(tokens, norm_gain.reshape(1, width), w_qkv, w_out, widths)


def solution(mesh):
    placed = (P(None, ("lon", "head"), None), P(), P(), P(), P())
    one_block = mesh.shape["lon"] == 8 and mesh.shape["head"] == 4
    return jax.shard_map(
        fused_device if one_block else per_device,
        mesh=mesh,
        in_specs=placed,
        out_specs=P(None, ("lon", "head"), None),
        check_vma=False,
    )
```

```python
import jax
import jax.numpy as jnp
from jax import lax
from jax.experimental import pallas as pl
from jax.experimental.pallas import tpu as pltpu
from jax.sharding import PartitionSpec as P

H = 8
HD = 128
LATITUDE_BANDS = 6
BLAT = 8
BLON = 16
REACH = 2
D = H * HD
BLOCK = BLAT * BLON
GROUP = LATITUDE_BANDS // 2
CHUNK = BLOCK // 4
SLOTS = 2 * REACH + 1
MESH = pl.DeviceIdType.MESH


def shifted(array, axis, by):
    count = lax.axis_size(axis)
    return lax.ppermute(array, axis, [(i, (i + by) % count) for i in range(count)])


def per_device(tokens, norm_gain, w_qkv, w_out, widths):
    lat_rows, lon_tok, width = tokens.shape
    n_head = lax.axis_size("head")
    pairs = LATITUDE_BANDS * H // n_head
    sector = lon_tok * n_head
    sblocks = sector // BLON
    block_len = BLAT * BLON
    scale = HD ** (-0.5)
    x32 = tokens.astype(jnp.float32)
    scale_rms = lax.rsqrt(jnp.mean(x32 * x32, axis=-1, keepdims=True) + 1e-05)
    normed = (x32 * scale_rms * norm_gain).astype(jnp.bfloat16)
    qkv = jnp.dot(normed.reshape(-1, width), w_qkv, preferred_element_type=jnp.float32).astype(
        jnp.bfloat16
    )
    qkv = (
        qkv.reshape(LATITUDE_BANDS, BLAT, lon_tok, 3, H, HD)
        .transpose(0, 4, 1, 2, 3, 5)
        .reshape(LATITUDE_BANDS * H, BLAT, lon_tok, 3 * HD)
    )
    mine = lax.all_to_all(qkv, "head", split_axis=0, concat_axis=2, tiled=True)
    blocks = (
        mine.reshape(pairs, BLAT, sblocks, BLON, 3 * HD)
        .transpose(0, 2, 1, 3, 4)
        .reshape(pairs, sblocks, block_len, 3 * HD)
    )
    query = blocks[..., :HD]
    keyval = blocks[..., HD:]
    pair_ids = lax.axis_index("head") * pairs + jnp.arange(pairs, dtype=jnp.int32)
    band_ids = pair_ids // H
    onehot = (band_ids[:, None] == jnp.arange(LATITUDE_BANDS, dtype=jnp.int32)[None, :]).astype(
        jnp.int32
    )
    band_widths = jnp.sum(onehot[:, :, None] * widths[None, :, :], axis=1)
    reach = lax.dynamic_slice_in_dim(band_widths, lax.axis_index("lon") * sblocks, sblocks, 1)
    q_index = jnp.arange(sblocks, dtype=jnp.int32)

    def attend(state, pieces, shift_blocks):
        top, total, accum = state
        keys = pieces[..., :HD]
        value_entries = pieces[..., HD:]
        scores = (
            jnp.einsum("pqtd,pkud->pqtku", query, keys, preferred_element_type=jnp.float32) * scale
        )
        offset = shift_blocks + q_index[None, :] - q_index[:, None]
        allowed = jnp.abs(offset)[None, :, :] <= reach[:, :, None]
        allowed = allowed[:, :, None, :, None]
        new_top = jnp.maximum(top, jnp.max(jnp.where(allowed, scores, -1e30), axis=(3, 4)))
        expo = jnp.where(allowed, jnp.exp(scores - new_top[..., None, None]), 0.0)
        factor = jnp.exp(top - new_top)
        total = total * factor + jnp.sum(expo, axis=(3, 4))
        update = jnp.einsum(
            "pqtku,pkud->pqtd",
            expo.astype(jnp.bfloat16),
            value_entries,
            preferred_element_type=jnp.float32,
        )
        accum = accum * factor[..., None] + update
        return (new_top, total, accum)

    start = (
        jnp.full((pairs, sblocks, block_len), -1e30, jnp.float32),
        jnp.zeros((pairs, sblocks, block_len), jnp.float32),
        jnp.zeros((pairs, sblocks, block_len, HD), jnp.float32),
    )
    state = attend(start, keyval, 0)
    travel = shifted(keyval, "lon", -REACH)
    state = attend(state, travel, REACH * sblocks)
    for step in range(1, 2 * REACH + 1):
        travel = shifted(travel, "lon", 1)
        distance = REACH - step
        if distance != 0:
            state = attend(state, travel, distance * sblocks)
    top, total, accum = state
    result = (accum / total[..., None]).astype(jnp.bfloat16)
    result = (
        result.reshape(pairs, sblocks, BLAT, BLON, HD)
        .transpose(0, 2, 1, 3, 4)
        .reshape(pairs, BLAT, sector, HD)
    )
    back = lax.all_to_all(result, "head", split_axis=2, concat_axis=0, tiled=True)
    back = (
        back.reshape(LATITUDE_BANDS, H, BLAT, lon_tok, HD)
        .transpose(0, 2, 3, 1, 4)
        .reshape(lat_rows * lon_tok, width)
    )
    proj = jnp.dot(back, w_out, preferred_element_type=jnp.float32)
    return (x32.reshape(-1, width) + proj).astype(jnp.bfloat16).reshape(lat_rows, lon_tok, width)


def fused_kernel(
    tok_hbm, gain_hbm, wqkv_hbm, wout_hbm, widths_hbm, out_ref,
    tok, gain, reach, buf, stage, wq, wo, qs, kv, att, back,
    wsem, x_send, x_recv, o_send, o_recv, c_send, c_recv, r_send, r_recv,
):
    n_lon = lax.axis_size("lon")
    lon, head = lax.axis_index("lon"), lax.axis_index("head")
    x, core = head // 2, head % 2
    y = lon % 2
    turn = 2 * y - 1
    far = (lax.rem(lon + 2 * turn + n_lon, n_lon), head)
    near = (lax.rem(lon - 2 * turn + n_lon, n_lon), head)
    pair = (lon - turn, head)
    sibling = (lon, 2 * x + 1 - core)
    across = (lon, 2 * (1 - x) + core)
    diagonal = (lon, 2 * (1 - x) + 1 - core)
    partners = [sibling, across, diagonal, far, near, pair]
    half_cols = H // 2 * HD

    barrier = pltpu.get_barrier_semaphore()
    for where in partners:
        pl.semaphore_signal(barrier, inc=1, device_id=where, device_id_type=MESH)

    first = [
        pltpu.make_async_copy(tok_hbm, tok, wsem.at[4]),
        pltpu.make_async_copy(gain_hbm, gain, wsem.at[5]),
    ]
    loads = []
    for i in range(3):
        cols = pl.ds(pl.multiple_of(i * H * HD + core * half_cols, 128), half_cols)
        loads.append(
            pltpu.make_async_copy(
                wqkv_hbm.at[:, cols], wq.at[:, pl.ds(i * half_cols, half_cols)], wsem.at[i]
            )
        )
    loads.append(pltpu.make_async_copy(wout_hbm, wo, wsem.at[3]))
    loads.append(pltpu.make_async_copy(widths_hbm, reach, wsem.at[6]))
    for load in first + loads:
        load.start()
    for load in first:
        load.wait()

    def normed(band):
        part = tok[pl.ds(band * BLAT, BLAT)].astype(jnp.float32).reshape(CHUNK, D)
        inv = lax.rsqrt(jnp.mean(part * part, axis=-1, keepdims=True) + 1e-05)
        return (part * inv * gain[...]).astype(jnp.bfloat16)

    def remote(src, dst, send, recv, where):
        return pltpu.make_async_remote_copy(
            src_ref=src, dst_ref=dst, send_sem=send, recv_sem=recv,
            device_id=where, device_id_type=MESH,
        )

    sent = []

    def begin(copy):
        copy.start()
        sent.append(copy)
        return copy

    def at(slot, j, piece):
        return buf.at[slot, j, core, x if piece == 0 else 1 - x]

    def move(slot_from, slot_to, j, piece, where):
        return begin(
            remote(
                at(slot_from, j, piece), at(slot_to, j, piece),
                o_send.at[slot_to, j, piece], o_recv.at[slot_to, j, piece], where,
            )
        )

    def share(slot, j):
        half = buf.at[slot, j, core]
        return begin(remote(half, half, c_send.at[slot, j], c_recv.at[slot, j], sibling))

    moves = {}

    def spread(j, piece):
        for slot, where in ((2, far), (1, pair)):
            moves[slot, j, piece] = move(0, slot, j, piece, where)

    def spread_near(j):
        for piece in range(2):
            moves[3, j, piece] = move(0, 3, j, piece, near)

    crossing = []
    for j in range(GROUP):
        stage[j] = normed((1 - x) * GROUP + j)
        if j == 0:
            pl.semaphore_wait(barrier, len(partners))
        crossing.append(
            begin(remote(stage.at[j], buf.at[0, j, core, x], x_send.at[j], x_recv.at[j], across))
        )
        buf[0, j, core, x] = normed(x * GROUP + j)
        spread(j, 0)
    shares = []
    for j in range(GROUP):
        crossing[j].wait_recv()
        spread(j, 1)
        shares.append(share(0, j))

    def project(slot, j, with_query):
        rows = jnp.concatenate(
            [buf[s, i].reshape(BLOCK, D) for s in slot for i in j], axis=0
        )
        start = 0 if with_query else half_cols
        made = jnp.dot(rows, wq[:, start:], preferred_element_type=jnp.float32).astype(
            jnp.bfloat16
        )
        n = 0
        for s in slot:
            for i in j:
                part = made[n * BLOCK : (n + 1) * BLOCK]
                if with_query:
                    qs[i] = part[:, :half_cols]
                    part = part[:, half_cols:]
                kv[i, pl.ds(s * BLOCK, BLOCK), :] = part
                n += 1

    for load in loads[:3]:
        load.wait()
    for copy in shares:
        copy.wait_recv()
    project((0,), range(GROUP), True)
    loads[4].wait()

    def relay(j):
        for piece in range(2):
            moves[2, j, piece].wait_recv()
            moves[4, j, piece] = move(2, 4, j, piece, pair)
        return share(2, j)

    def collect(slot, j):
        for piece in range(2):
            moves[slot, j, piece].wait_recv()
        return share(slot, j)

    def attend(j, h, low, high, dist):
        cols = pl.ds(h * HD, HD)
        rows = pl.ds(low * BLOCK, (high - low) * BLOCK)
        scores = lax.dot_general(
            qs[j, :, cols], kv[j, rows, cols], (((1,), (1,)), ((), ())),
            preferred_element_type=jnp.float32,
        )
        scores = jnp.where(dist <= reach[x * GROUP + j, lon], scores * HD ** (-0.5), -1e30)
        top = jnp.max(scores, axis=1, keepdims=True)

        def weigh(new_top):
            expo = jnp.exp(scores - new_top)
            value = jnp.dot(
                expo.astype(jnp.bfloat16), kv[j, rows, pl.ds(half_cols + h * HD, HD)],
                preferred_element_type=jnp.float32,
            )
            return jnp.sum(expo, axis=1, keepdims=True), value

        return top, weigh

    block = lax.broadcasted_iota(jnp.int32, (1, 3 * BLOCK), 1) // BLOCK
    dist_early = block
    dist_late = 2 - block[:, : 2 * BLOCK]
    returns = {}

    def finish(js):
        bands = [chip * GROUP + j for chip in range(2) for j in js]
        for j in js:
            for copy in returns[j]:
                copy.wait_recv()
        rows = jnp.concatenate(
            [
                jnp.concatenate([back[c, b * CHUNK : (b + 1) * CHUNK] for b in bands], axis=0)
                for c in range(2)
            ],
            axis=1,
        )
        proj = jnp.dot(rows, wo[...], preferred_element_type=jnp.float32)
        for n, b in enumerate(bands):
            held = tok[b * BLAT : (b + 1) * BLAT].astype(jnp.float32)
            add = proj[n * CHUNK : (n + 1) * CHUNK]
            out_ref[b * CHUNK : (b + 1) * CHUNK] = (held.reshape(CHUNK, D) + add).astype(
                jnp.bfloat16
            )

    states = {}

    def early(j):
        for h in range(H // 2):
            top, weigh = attend(j, h, 0, 3, dist_early)
            states[j, h] = (top, *weigh(top))

    def late(j):
        for h in range(H // 2):
            top, total, value = states[j, h]
            late_top, weigh = attend(j, h, 3, 5, dist_late)
            new_top = jnp.maximum(top, late_top)
            factor = jnp.exp(top - new_top)
            late_total, late_value = weigh(new_top)
            value = value * factor + late_value
            total = total * factor + late_total
            att[j, :, pl.ds(h * HD, HD)] = (value / total).astype(jnp.bfloat16)

    far_shares = []
    for j in range(GROUP):
        far_shares.append(relay(j))
        if j > 0:
            spread_near(j - 1)
    spread_near(GROUP - 1)
    pair_shares = [collect(1, j) for j in range(GROUP)]
    for copy in pair_shares:
        copy.wait_recv()
    project((1,), range(GROUP), False)
    for copy in far_shares:
        copy.wait_recv()
    project((2,), range(GROUP), False)
    early(0)
    for j in range(GROUP):
        late_shares = [collect(3, j), collect(4, j)]
        if j + 1 < GROUP:
            early(j + 1)
        else:
            loads[3].wait()
            finish(range(GROUP - 1))
        for copy in late_shares:
            copy.wait_recv()
        project((3, 4), (j,), False)
        late(j)
        rows = pl.ds(pl.multiple_of((x * GROUP + j) * CHUNK, CHUNK), CHUNK)
        returns[j] = []
        for kind, (where, to_x, to_core) in enumerate(
            ((across, 1 - x, core), (diagonal, 1 - x, 1 - core), (sibling, x, 1 - core))
        ):
            piece = pl.ds(pl.multiple_of((to_core * 2 + to_x) * CHUNK, CHUNK), CHUNK)
            returns[j].append(
                begin(
                    remote(
                        att.at[j, piece], back.at[core, rows],
                        r_send.at[j, kind], r_recv.at[j, kind], where,
                    )
                )
            )
        mine = pl.ds(pl.multiple_of((core * 2 + x) * CHUNK, CHUNK), CHUNK)
        back[core, rows] = att[j, mine]

    finish((GROUP - 1,))
    for copy in sent:
        copy.wait_send()


def fused_device(tokens, norm_gain, w_qkv, w_out, widths):
    lat_rows, lon_tok, width = tokens.shape
    count = lat_rows * lon_tok
    half_cols = H // 2 * HD
    dma = pltpu.SemaphoreType.DMA
    hbm = pl.BlockSpec(memory_space=pltpu.HBM)
    out = pl.pallas_call(
        fused_kernel,
        out_shape=jax.ShapeDtypeStruct((count, width), jnp.bfloat16),
        in_specs=[hbm] * 5,
        out_specs=pl.BlockSpec(memory_space=pltpu.VMEM),
        scratch_shapes=[
            pltpu.VMEM(tokens.shape, jnp.bfloat16),
            pltpu.VMEM((1, width), jnp.float32),
            pltpu.SMEM(widths.shape, jnp.int32),
            pltpu.VMEM((SLOTS, GROUP, 2, 2, CHUNK, width), jnp.bfloat16),
            pltpu.VMEM((GROUP, CHUNK, width), jnp.bfloat16),
            pltpu.VMEM((width, 3 * half_cols), jnp.bfloat16),
            pltpu.VMEM((width, width), jnp.bfloat16),
            pltpu.VMEM((GROUP, BLOCK, half_cols), jnp.bfloat16),
            pltpu.VMEM((GROUP, SLOTS * BLOCK, 2 * half_cols), jnp.bfloat16),
            pltpu.VMEM((GROUP, BLOCK, half_cols), jnp.bfloat16),
            pltpu.VMEM((2, count, half_cols), jnp.bfloat16),
            dma((7,)),
            dma((GROUP,)),
            dma((GROUP,)),
            dma((SLOTS, GROUP, 2)),
            dma((SLOTS, GROUP, 2)),
            dma((SLOTS, GROUP)),
            dma((SLOTS, GROUP)),
            dma((GROUP, 3)),
            dma((GROUP, 3)),
        ],
        compiler_params=pltpu.CompilerParams(
            collective_id=0, has_side_effects=True, vmem_limit_bytes=56 * 1024 * 1024
        ),
    )(tokens, norm_gain.reshape(1, width), w_qkv, w_out, widths)
    return out.reshape(lat_rows, lon_tok, width)


def solution(mesh):
    placed = (P(None, ("lon", "head"), None), P(), P(), P(), P())
    one_block = mesh.shape["lon"] == 8 and mesh.shape["head"] == 4
    return jax.shard_map(
        fused_device if one_block else per_device,
        mesh=mesh,
        in_specs=placed,
        out_specs=P(None, ("lon", "head"), None),
        check_vma=False,
    )
```

```python
import jax
import jax.numpy as jnp
from jax import lax
from jax.experimental import pallas as pl
from jax.experimental.pallas import tpu as pltpu
from jax.sharding import PartitionSpec as P

H = 8
HD = 128
LATITUDE_BANDS = 6
BLAT = 8
BLON = 16
REACH = 2
D = H * HD
BLOCK = BLAT * BLON
GROUP = LATITUDE_BANDS // 2
CHUNK = BLOCK // 4
SLOTS = 2 * REACH + 1
MESH = pl.DeviceIdType.MESH


def shifted(array, axis, by):
    count = lax.axis_size(axis)
    return lax.ppermute(array, axis, [(i, (i + by) % count) for i in range(count)])


def per_device(tokens, norm_gain, w_qkv, w_out, widths):
    lat_rows, lon_tok, width = tokens.shape
    n_head = lax.axis_size("head")
    pairs = LATITUDE_BANDS * H // n_head
    sector = lon_tok * n_head
    sblocks = sector // BLON
    block_len = BLAT * BLON
    scale = HD ** (-0.5)
    x32 = tokens.astype(jnp.float32)
    scale_rms = lax.rsqrt(jnp.mean(x32 * x32, axis=-1, keepdims=True) + 1e-05)
    normed = (x32 * scale_rms * norm_gain).astype(jnp.bfloat16)
    qkv = jnp.dot(normed.reshape(-1, width), w_qkv, preferred_element_type=jnp.float32).astype(
        jnp.bfloat16
    )
    qkv = (
        qkv.reshape(LATITUDE_BANDS, BLAT, lon_tok, 3, H, HD)
        .transpose(0, 4, 1, 2, 3, 5)
        .reshape(LATITUDE_BANDS * H, BLAT, lon_tok, 3 * HD)
    )
    mine = lax.all_to_all(qkv, "head", split_axis=0, concat_axis=2, tiled=True)
    blocks = (
        mine.reshape(pairs, BLAT, sblocks, BLON, 3 * HD)
        .transpose(0, 2, 1, 3, 4)
        .reshape(pairs, sblocks, block_len, 3 * HD)
    )
    query = blocks[..., :HD]
    keyval = blocks[..., HD:]
    pair_ids = lax.axis_index("head") * pairs + jnp.arange(pairs, dtype=jnp.int32)
    band_ids = pair_ids // H
    onehot = (band_ids[:, None] == jnp.arange(LATITUDE_BANDS, dtype=jnp.int32)[None, :]).astype(
        jnp.int32
    )
    band_widths = jnp.sum(onehot[:, :, None] * widths[None, :, :], axis=1)
    reach = lax.dynamic_slice_in_dim(band_widths, lax.axis_index("lon") * sblocks, sblocks, 1)
    q_index = jnp.arange(sblocks, dtype=jnp.int32)

    def attend(state, pieces, shift_blocks):
        top, total, accum = state
        keys = pieces[..., :HD]
        value_entries = pieces[..., HD:]
        scores = (
            jnp.einsum("pqtd,pkud->pqtku", query, keys, preferred_element_type=jnp.float32) * scale
        )
        offset = shift_blocks + q_index[None, :] - q_index[:, None]
        allowed = jnp.abs(offset)[None, :, :] <= reach[:, :, None]
        allowed = allowed[:, :, None, :, None]
        new_top = jnp.maximum(top, jnp.max(jnp.where(allowed, scores, -1e30), axis=(3, 4)))
        expo = jnp.where(allowed, jnp.exp(scores - new_top[..., None, None]), 0.0)
        factor = jnp.exp(top - new_top)
        total = total * factor + jnp.sum(expo, axis=(3, 4))
        update = jnp.einsum(
            "pqtku,pkud->pqtd",
            expo.astype(jnp.bfloat16),
            value_entries,
            preferred_element_type=jnp.float32,
        )
        accum = accum * factor[..., None] + update
        return (new_top, total, accum)

    start = (
        jnp.full((pairs, sblocks, block_len), -1e30, jnp.float32),
        jnp.zeros((pairs, sblocks, block_len), jnp.float32),
        jnp.zeros((pairs, sblocks, block_len, HD), jnp.float32),
    )
    state = attend(start, keyval, 0)
    travel = shifted(keyval, "lon", -REACH)
    state = attend(state, travel, REACH * sblocks)
    for step in range(1, 2 * REACH + 1):
        travel = shifted(travel, "lon", 1)
        distance = REACH - step
        if distance != 0:
            state = attend(state, travel, distance * sblocks)
    top, total, accum = state
    result = (accum / total[..., None]).astype(jnp.bfloat16)
    result = (
        result.reshape(pairs, sblocks, BLAT, BLON, HD)
        .transpose(0, 2, 1, 3, 4)
        .reshape(pairs, BLAT, sector, HD)
    )
    back = lax.all_to_all(result, "head", split_axis=2, concat_axis=0, tiled=True)
    back = (
        back.reshape(LATITUDE_BANDS, H, BLAT, lon_tok, HD)
        .transpose(0, 2, 3, 1, 4)
        .reshape(lat_rows * lon_tok, width)
    )
    proj = jnp.dot(back, w_out, preferred_element_type=jnp.float32)
    return (x32.reshape(-1, width) + proj).astype(jnp.bfloat16).reshape(lat_rows, lon_tok, width)


def fused_kernel(
    tok_hbm, gain_hbm, wqkv_hbm, wout_hbm, widths_hbm, out_ref,
    tok, gain, reach, buf, stage, wq, wo, qs, kv, att, back,
    wsem, x_send, x_recv, o_send, o_recv, c_send, c_recv, r_send, r_recv,
):
    n_lon = lax.axis_size("lon")
    lon, head = lax.axis_index("lon"), lax.axis_index("head")
    x, core = head // 2, head % 2
    y = lon % 2
    turn = 2 * y - 1
    far = (lax.rem(lon + 2 * turn + n_lon, n_lon), head)
    near = (lax.rem(lon - 2 * turn + n_lon, n_lon), head)
    pair = (lon - turn, head)
    sibling = (lon, 2 * x + 1 - core)
    across = (lon, 2 * (1 - x) + core)
    diagonal = (lon, 2 * (1 - x) + 1 - core)
    partners = [sibling, across, diagonal, far, near, pair]
    half_cols = H // 2 * HD

    barrier = pltpu.get_barrier_semaphore()
    for where in partners:
        pl.semaphore_signal(barrier, inc=1, device_id=where, device_id_type=MESH)

    first = [
        pltpu.make_async_copy(tok_hbm, tok, wsem.at[4]),
        pltpu.make_async_copy(gain_hbm, gain, wsem.at[5]),
    ]
    loads = []
    for i in range(3):
        cols = pl.ds(pl.multiple_of(i * H * HD + core * half_cols, 128), half_cols)
        loads.append(
            pltpu.make_async_copy(
                wqkv_hbm.at[:, cols], wq.at[:, pl.ds(i * half_cols, half_cols)], wsem.at[i]
            )
        )
    loads.append(pltpu.make_async_copy(wout_hbm, wo, wsem.at[3]))
    loads.append(pltpu.make_async_copy(widths_hbm, reach, wsem.at[6]))
    for load in first + loads:
        load.start()
    for load in first:
        load.wait()

    def normed(band):
        part = tok[pl.ds(band * BLAT, BLAT)].astype(jnp.float32).reshape(CHUNK, D)
        inv = lax.rsqrt(jnp.mean(part * part, axis=-1, keepdims=True) + 1e-05)
        return (part * inv * gain[...]).astype(jnp.bfloat16)

    def remote(src, dst, send, recv, where):
        return pltpu.make_async_remote_copy(
            src_ref=src, dst_ref=dst, send_sem=send, recv_sem=recv,
            device_id=where, device_id_type=MESH,
        )

    sent = []

    def begin(copy):
        copy.start()
        sent.append(copy)
        return copy

    def at(slot, j, piece):
        return buf.at[slot, j, core, x if piece == 0 else 1 - x]

    def move(slot_from, slot_to, j, piece, where):
        return begin(
            remote(
                at(slot_from, j, piece), at(slot_to, j, piece),
                o_send.at[slot_to, j, piece], o_recv.at[slot_to, j, piece], where,
            )
        )

    def share(slot, j):
        half = buf.at[slot, j, core]
        return begin(remote(half, half, c_send.at[slot, j], c_recv.at[slot, j], sibling))

    moves = {}

    def spread(j, piece):
        for slot, where in ((2, far), (1, pair)):
            moves[slot, j, piece] = move(0, slot, j, piece, where)

    def spread_near(j):
        for piece in range(2):
            moves[3, j, piece] = move(0, 3, j, piece, near)

    crossing = []
    for j in range(GROUP):
        stage[j] = normed((1 - x) * GROUP + j)
        if j == 0:
            pl.semaphore_wait(barrier, len(partners))
        crossing.append(
            begin(remote(stage.at[j], buf.at[0, j, core, x], x_send.at[j], x_recv.at[j], across))
        )
        buf[0, j, core, x] = normed(x * GROUP + j)
        spread(j, 0)
    shares = []
    for j in range(GROUP):
        crossing[j].wait_recv()
        spread(j, 1)
        shares.append(share(0, j))

    def project(slot, j, with_query):
        rows = jnp.concatenate(
            [buf[s, i].reshape(BLOCK, D) for s in slot for i in j], axis=0
        )
        start = 0 if with_query else half_cols
        made = jnp.dot(rows, wq[:, start:], preferred_element_type=jnp.float32).astype(
            jnp.bfloat16
        )
        n = 0
        for s in slot:
            for i in j:
                part = made[n * BLOCK : (n + 1) * BLOCK]
                if with_query:
                    qs[i] = part[:, :half_cols]
                    part = part[:, half_cols:]
                kv[i, pl.ds(s * BLOCK, BLOCK), :] = part
                n += 1

    for load in loads[:3]:
        load.wait()
    for copy in shares:
        copy.wait_recv()
    project((0,), range(GROUP), True)
    loads[4].wait()

    def relay(j):
        for piece in range(2):
            moves[2, j, piece].wait_recv()
            moves[4, j, piece] = move(2, 4, j, piece, pair)
        return share(2, j)

    def collect(slot, j):
        for piece in range(2):
            moves[slot, j, piece].wait_recv()
        return share(slot, j)

    def attend(j, h, low, high, dist):
        cols = pl.ds(h * HD, HD)
        rows = pl.ds(low * BLOCK, (high - low) * BLOCK)
        scores = lax.dot_general(
            qs[j, :, cols], kv[j, rows, cols], (((1,), (1,)), ((), ())),
            preferred_element_type=jnp.float32,
        )
        scores = jnp.where(dist <= reach[x * GROUP + j, lon], scores * HD ** (-0.5), -1e30)
        top = jnp.max(scores, axis=1, keepdims=True)

        def weigh(new_top):
            expo = jnp.exp(scores - new_top)
            value = jnp.dot(
                expo.astype(jnp.bfloat16), kv[j, rows, pl.ds(half_cols + h * HD, HD)],
                preferred_element_type=jnp.float32,
            )
            return jnp.sum(expo, axis=1, keepdims=True), value

        return top, weigh

    block = lax.broadcasted_iota(jnp.int32, (1, 3 * BLOCK), 1) // BLOCK
    dist_early = block
    dist_late = 2 - block[:, : 2 * BLOCK]
    returns = {}

    def finish(js):
        bands = [chip * GROUP + j for chip in range(2) for j in js]
        for j in js:
            for copy in returns[j]:
                copy.wait_recv()
        rows = jnp.concatenate(
            [
                jnp.concatenate([back[c, b * CHUNK : (b + 1) * CHUNK] for b in bands], axis=0)
                for c in range(2)
            ],
            axis=1,
        )
        proj = jnp.dot(rows, wo[...], preferred_element_type=jnp.float32)
        for n, b in enumerate(bands):
            held = tok[b * BLAT : (b + 1) * BLAT].astype(jnp.float32)
            add = proj[n * CHUNK : (n + 1) * CHUNK]
            out_ref[b * CHUNK : (b + 1) * CHUNK] = (held.reshape(CHUNK, D) + add).astype(
                jnp.bfloat16
            )

    states = {}

    def early(j):
        for h in range(H // 2):
            top, weigh = attend(j, h, 0, 3, dist_early)
            states[j, h] = (top, *weigh(top))

    def late(j):
        for h in range(H // 2):
            top, total, value = states[j, h]
            late_top, weigh = attend(j, h, 3, 5, dist_late)
            new_top = jnp.maximum(top, late_top)
            factor = jnp.exp(top - new_top)
            late_total, late_value = weigh(new_top)
            value = value * factor + late_value
            total = total * factor + late_total
            att[j, :, pl.ds(h * HD, HD)] = (value / total).astype(jnp.bfloat16)

    far_shares = []
    for j in range(GROUP):
        far_shares.append(relay(j))
        spread_near(j)
    pair_shares = [collect(1, j) for j in range(GROUP)]
    for copy in pair_shares:
        copy.wait_recv()
    project((1,), range(GROUP), False)
    for copy in far_shares:
        copy.wait_recv()
    project((2,), range(GROUP), False)
    early(0)
    for j in range(GROUP):
        late_shares = [collect(3, j), collect(4, j)]
        if j + 1 < GROUP:
            early(j + 1)
        else:
            loads[3].wait()
            finish(range(GROUP - 1))
        for copy in late_shares:
            copy.wait_recv()
        project((3, 4), (j,), False)
        late(j)
        rows = pl.ds(pl.multiple_of((x * GROUP + j) * CHUNK, CHUNK), CHUNK)
        returns[j] = []
        for kind, (where, to_x, to_core) in enumerate(
            ((across, 1 - x, core), (diagonal, 1 - x, 1 - core), (sibling, x, 1 - core))
        ):
            piece = pl.ds(pl.multiple_of((to_core * 2 + to_x) * CHUNK, CHUNK), CHUNK)
            returns[j].append(
                begin(
                    remote(
                        att.at[j, piece], back.at[core, rows],
                        r_send.at[j, kind], r_recv.at[j, kind], where,
                    )
                )
            )
        mine = pl.ds(pl.multiple_of((core * 2 + x) * CHUNK, CHUNK), CHUNK)
        back[core, rows] = att[j, mine]

    finish((GROUP - 1,))
    for copy in sent:
        copy.wait_send()


def fused_device(tokens, norm_gain, w_qkv, w_out, widths):
    lat_rows, lon_tok, width = tokens.shape
    count = lat_rows * lon_tok
    half_cols = H // 2 * HD
    dma = pltpu.SemaphoreType.DMA
    hbm = pl.BlockSpec(memory_space=pltpu.HBM)
    out = pl.pallas_call(
        fused_kernel,
        out_shape=jax.ShapeDtypeStruct((count, width), jnp.bfloat16),
        in_specs=[hbm] * 5,
        out_specs=pl.BlockSpec(memory_space=pltpu.VMEM),
        scratch_shapes=[
            pltpu.VMEM(tokens.shape, jnp.bfloat16),
            pltpu.VMEM((1, width), jnp.float32),
            pltpu.SMEM(widths.shape, jnp.int32),
            pltpu.VMEM((SLOTS, GROUP, 2, 2, CHUNK, width), jnp.bfloat16),
            pltpu.VMEM((GROUP, CHUNK, width), jnp.bfloat16),
            pltpu.VMEM((width, 3 * half_cols), jnp.bfloat16),
            pltpu.VMEM((width, width), jnp.bfloat16),
            pltpu.VMEM((GROUP, BLOCK, half_cols), jnp.bfloat16),
            pltpu.VMEM((GROUP, SLOTS * BLOCK, 2 * half_cols), jnp.bfloat16),
            pltpu.VMEM((GROUP, BLOCK, half_cols), jnp.bfloat16),
            pltpu.VMEM((2, count, half_cols), jnp.bfloat16),
            dma((7,)),
            dma((GROUP,)),
            dma((GROUP,)),
            dma((SLOTS, GROUP, 2)),
            dma((SLOTS, GROUP, 2)),
            dma((SLOTS, GROUP)),
            dma((SLOTS, GROUP)),
            dma((GROUP, 3)),
            dma((GROUP, 3)),
        ],
        compiler_params=pltpu.CompilerParams(
            collective_id=0, has_side_effects=True, vmem_limit_bytes=56 * 1024 * 1024
        ),
    )(tokens, norm_gain.reshape(1, width), w_qkv, w_out, widths)
    return out.reshape(lat_rows, lon_tok, width)


def solution(mesh):
    placed = (P(None, ("lon", "head"), None), P(), P(), P(), P())
    one_block = mesh.shape["lon"] == 8 and mesh.shape["head"] == 4
    return jax.shard_map(
        fused_device if one_block else per_device,
        mesh=mesh,
        in_specs=placed,
        out_specs=P(None, ("lon", "head"), None),
        check_vma=False,
    )
```
